32 devices in a mesh: seg: 4 (over y, x), bond: 8 (over z, core).
Axes of the slice: x: 2, y: 2, z: 4, core: 2. Of those that a mesh axis runs over, the one named last changes fastest.
Arguments:
- sites: float32 [4, 2, 8192, 8192], P('seg', None, 'bond'), may hold values from -0.6629126 to 0.6629126, as said below
- boundary: float32 [8192], P('bond'), may hold values from -6 to 6
- bits: int32 [32, 4], P(None, 'seg'), may hold values from 0 to 1
- order: int32 [32], replicated, may hold values from 0 to 31, each once
Outputs:
- probs: float32 [32, 4], P(None, 'seg')
The draws below stay inside these ranges and needn't reach their ends.
Inputs may be any that keep to these rules, and one draw needn't show every extreme that they name: `order`: each slot number appears once. `sites`: real entries.
All inputs are finite; a program needn't handle non-finite values.
Results may differ from the reference program's by a relative error of at most 0.0001.
Values sent between devices are 32-bit elements; how exact they have to be, the bound alone decides.
No kernel may reach another device: no remote copies, remote signals or barrier semaphores. Data moves between devices by JAX's collectives and lax.ppermute only.
A program may use at most 128 MiB of HBM per device.

```python
import math
import jax
import jax.numpy as jnp
from jax import lax

D = 8192
ROWS = 32
SITES = 4


def draw_sites(key, part):
    noise_key = jax.random.fold_in(key, 11)
    row_key = jax.random.fold_in(key, 23)
    col_key = jax.random.fold_in(key, 37)
    shape = (SITES, 2, D, D)
    noise = jax.random.truncated_normal(noise_key, -6.0, 6.0, shape, jnp.float32)
    row_scale = jnp.exp(jax.random.uniform(row_key, (SITES, 2, D, 1), jnp.float32, 0.0, math.log(10.0)))
    col_scale = jnp.exp(jax.random.uniform(col_key, (SITES, 2, 1, D), jnp.float32, 0.0, math.log(10.0)))
    return noise * row_scale * col_scale * (0.1 / math.sqrt(D))


def with_ends(array, stream_key, low, top_value):
    longest = array.shape.index(max(array.shape))
    spots = []
    for shift in (0, 1):
        where = [jax.random.randint(jax.random.fold_in(stream_key, axis), (), 0, length) for axis, length in enumerate(array.shape)]
        where[longest] = (where[longest] + shift) % array.shape[longest]
        spots.append(tuple(where))
    return array.at[spots[0]].set(low).at[spots[1]].set(top_value)


def block_scale(key, shape, cuts, smallest, top_value):
    def one(position, blocks):
        steps = jax.random.uniform(jax.random.fold_in(jax.random.fold_in(key, 6), position), (blocks,), jnp.float32, smallest / len(cuts), top_value / len(cuts))
        return jnp.repeat(jnp.exp(steps), shape[position] // blocks).reshape((-1,) + (1,) * (len(shape) - position - 1))

    factor_of = one(*cuts[0])
    for cut in cuts[1:]:
        factor_of = factor_of * one(*cut)
    return factor_of


def scatter_about(key, dims, width, bound, cuts=(), dtype=jnp.bfloat16):
    values = width * jax.random.normal(key, dims, jnp.float32)
    if cuts:
        values = values * block_scale(key, dims, cuts, -0.22, 0.18)
    return jnp.clip(values, -bound, bound).astype(dtype)


def setup_inputs(seed: int = 0) -> dict:
    arg_keys = jax.random.split(jax.random.key(seed), 5)
    sites = draw_sites(jax.random.fold_in(arg_keys[4], 71), 0)
    boundary = scatter_about(arg_keys[1], (D,), 1.0, 6.0, ((0, 8),), jnp.float32)
    bits = with_ends(jax.random.randint(arg_keys[2], (ROWS, SITES), 0, 2), jax.random.fold_in(arg_keys[2], 1), 0, 1).astype(jnp.int32)
    order = jax.random.permutation(arg_keys[3], ROWS).astype(jnp.int32)
    return dict(sites=sites, boundary=boundary, bits=bits, order=order)


EPSILON = 1e-06

def reference(sites, boundary, bits, order):
    slot_bits = jnp.take(bits, order, axis=0)
    env = jnp.broadcast_to(boundary[None, :], (ROWS, D)).astype(jnp.float32)
    columns = []
    for k in range(SITES):
        amp_zero = jnp.dot(env, sites[k, 0], precision=lax.Precision.HIGHEST, preferred_element_type=jnp.float32)
        amp_one = jnp.dot(env, sites[k, 1], precision=lax.Precision.HIGHEST, preferred_element_type=jnp.float32)
        mean_zero = lax.optimization_barrier(jnp.mean(amp_zero * amp_zero, axis=1)) + EPSILON
        mean_one = lax.optimization_barrier(jnp.mean(amp_one * amp_one, axis=1)) + EPSILON
        picked = slot_bits[:, k] == 1
        weight = jnp.where(picked, mean_one, mean_zero)
        columns.append(weight / (mean_zero + mean_one))
        chosen = jnp.where(picked[:, None], amp_one, amp_zero)
        env = chosen * lax.rsqrt(weight)[:, None]
    return jnp.stack(columns, axis=1)
```

```python
import functools

import jax
import jax.numpy as jnp
from jax import lax
from jax.experimental import pallas as pl
from jax.experimental.pallas import tpu as pltpu
from jax.sharding import PartitionSpec as P

EPSILON = 1e-06
AXES = ("seg", "bond")
LANES = 128
MIB = 2**20
HELD_BYTES = 48 * MIB
BLOCK = 2048
RING = 4
SCOPE = 12 * MIB
F32 = jnp.float32
BF16 = jnp.bfloat16
VMEM = pl.BlockSpec(memory_space=pltpu.VMEM)
ANY = pl.BlockSpec(memory_space=pl.ANY)


class Sizes:
    def __init__(self, sites, bits):
        assert sites.shape[0] == 1
        self.segs = lax.axis_size("seg")
        self.bonds = lax.axis_size("bond")
        self.half = self.bonds // 2
        self.left, self.right = sites.shape[2], sites.shape[3]
        self.chunk = self.right // self.bonds
        assert self.chunk == self.left and self.bonds % 2 == 0
        self.rows = bits.shape[0]
        self.most = 2**self.segs
        need = max(2 * self.most - 2, self.rows * self.segs)
        self.extra = -(-need // LANES) * LANES
        self.width = self.chunk + self.extra
        self.block = min(BLOCK, self.right)
        self.per_bit = self.right // self.block
        self.blocks = 2 * self.per_bit
        self.held = min(self.blocks, HELD_BYTES // (self.left * self.block * 4))
        self.piece = min(512, self.chunk)
        self.pieces = self.block // self.piece

    def place(self, column):
        owner = column // self.chunk
        return owner // 2, owner % 2


def split(x):
    high = x.astype(BF16)
    return high, (x - high.astype(F32)).astype(BF16)


def piece_copy(sz, site, ring, sems, index):
    per = sz.right // sz.piece
    column = pl.multiple_of((index % per) * sz.piece, sz.piece)
    slot = index % RING
    return pltpu.make_async_copy(
        site.at[index // per, :, pl.ds(column, sz.piece)], ring.at[slot], sems.at[slot]
    )


def bit_row(sz, bits_ref, group, extra):
    mine = bits_ref[...].astype(F32)
    wide = jnp.concatenate([mine] * (sz.extra // sz.rows), axis=1) if sz.extra > sz.rows else mine
    lane = lax.broadcasted_iota(jnp.int32, (1, sz.extra), 1)
    return extra + jnp.where(lane // sz.rows == group, wide, 0.0)


def first_kernel(sz, bits_ref, start_ref, site, keep, give, fin_keep, fin_give, *rest):
    highs, lows = rest[: sz.held], rest[sz.held : 2 * sz.held]
    ring, spread, out, sems = rest[2 * sz.held :]
    group = lax.axis_index("seg")
    bond = lax.axis_index("bond")
    core = bond % 2
    copy = functools.partial(piece_copy, sz, site, ring, sems)

    @pl.when(group == 0)
    def _():
        total = 2 * sz.right // sz.piece
        for i in range(RING):
            copy(i).start()
        turned = jnp.transpose(jnp.broadcast_to(start_ref[...], (8, sz.left)))
        spread[...] = jnp.broadcast_to(turned[:, 0:1], (sz.left, LANES))
        out[...] = jnp.zeros_like(out)
        per = sz.right // sz.piece
        for bit in range(2):

            def body(i, _):
                index = bit * per + i
                slot = index % RING
                copy(index).wait()
                sums = [None] * (sz.piece // LANES)
                for g in range(sz.left // 8):
                    env = spread[g * 8 : (g + 1) * 8, :]
                    for j in range(len(sums)):
                        term = ring[slot, g * 8 : (g + 1) * 8, j * LANES : (j + 1) * LANES] * env
                        sums[j] = term if g == 0 else sums[j] + term

                @pl.when(index + RING < total)
                def _():
                    copy(index + RING).start()

                column = i * sz.piece
                pair, side = sz.place(column)
                offset = pl.multiple_of(column % sz.chunk, sz.piece)
                row = jnp.concatenate([jnp.sum(s, axis=0, keepdims=True) for s in sums], axis=1)
                out[side, pair, bit : bit + 1, pl.ds(offset, sz.piece)] = row
                return 0

            lax.fori_loop(0, per, body, 0)
        none = jnp.zeros((1, sz.extra), F32)
        row = jnp.where(bond == 0, bit_row(sz, bits_ref, group, none), 0.0)
        for side in range(2):
            for pair in range(sz.half):
                out[side, pair, 1:2, sz.chunk :] = row
        keep[...] = out[core]
        give[...] = out[1 - core]
        fin_keep[...] = jnp.zeros_like(fin_keep)
        fin_give[...] = jnp.zeros_like(fin_give)
        fin_keep[:, 0:2, :] = out[core]
        fin_give[:, 0:2, :] = out[1 - core]

    @pl.when(group != 0)
    def _():
        total = sz.held * sz.pieces
        for i in range(min(RING, total)):
            copy(i).start()
        for b in range(sz.held):

            def body(i, _):
                index = b * sz.pieces + i
                slot = index % RING
                copy(index).wait()
                high, low = split(ring[slot])
                column = pl.multiple_of(i * sz.piece, sz.piece)
                highs[b][:, pl.ds(column, sz.piece)] = high
                lows[b][:, pl.ds(column, sz.piece)] = low

                @pl.when(index + RING < total)
                def _():
                    copy(index + RING).start()

                return 0

            lax.fori_loop(0, sz.pieces, body, 0)
        keep[...] = jnp.zeros_like(keep)
        give[...] = jnp.zeros_like(give)
        fin_keep[...] = jnp.zeros_like(fin_keep)
        fin_give[...] = jnp.zeros_like(fin_give)


def place_norms(sz, env, level):
    norms = jnp.sum(env * env, axis=1, keepdims=True)
    shape = (env.shape[0], sz.extra)
    lane = lax.broadcasted_iota(jnp.int32, shape, 1)
    row = lax.broadcasted_iota(jnp.int32, shape, 0)
    first = 2 * lax.shift_left(1, level) - 2
    return jnp.sum(jnp.where(lane == row + first, norms, 0.0), axis=0, keepdims=True)


def site_kernel(sz, step, *refs):
    last = step == sz.segs - 1
    refs = list(refs)
    bits_ref, site = refs[:2]
    messages = refs[2 : 2 + sz.half]
    refs = refs[2 + sz.half :]
    highs, lows = refs[: sz.held], refs[sz.held : 2 * sz.held]
    old_keep, old_give = refs[2 * sz.held : 2 * sz.held + 2]
    refs = refs[2 * sz.held + 2 :]
    if last:
        fin_keep, fin_give = refs[:2]
        refs = refs[2:]
    else:
        keep, give, fin_keep, fin_give = refs[:4]
        refs = refs[4:]
    ring, lhs_ref, out, sems = refs
    group = lax.axis_index("seg")
    bond = lax.axis_index("bond")
    core = bond % 2
    rows = 2**step
    copy = functools.partial(piece_copy, sz, site, ring, sems)

    @pl.when(group == step)
    def _():
        streamed = range(sz.held * sz.pieces, sz.blocks * sz.pieces)
        for i in streamed[:RING]:
            copy(i).start()
        total = messages[0][...]
        for m in messages[1:]:
            total = total + m[...]
        env = total[:, : sz.chunk]
        norms = total[0:1, sz.chunk :]
        taken = total[1:2, sz.chunk :]
        high, low = split(env)
        lhs_ref[...] = jnp.zeros_like(lhs_ref)
        lhs_ref[0:rows, :] = high.astype(F32)
        lhs_ref[rows : 2 * rows, :] = low.astype(F32)
        lhs = lhs_ref[...].astype(BF16)
        out[...] = jnp.zeros_like(out)

        def product(w_high, w_low, bit, column, columns):
            acc = jnp.dot(lhs, w_high, preferred_element_type=F32)
            acc = acc + jnp.dot(lhs, w_low, preferred_element_type=F32)
            amp = acc[0:rows] + acc[rows : 2 * rows]
            size = min(columns, sz.chunk)
            for start in range(0, columns, size):
                pair, side = sz.place(column + start)
                offset = (column + start) % sz.chunk
                out[side, pair, bit * rows : (bit + 1) * rows, offset : offset + size] = amp[
                    :, start : start + size
                ]

        def stream(index):
            copy(index).wait()
            w_high, w_low = split(ring[index % RING])
            per = sz.right // sz.piece
            product(w_high, w_low, index // per, (index % per) * sz.piece, sz.piece)
            if index + RING in streamed:
                copy(index + RING).start()

        waiting = list(streamed)
        share = -(-len(waiting) // max(sz.held, 1))
        for b in range(sz.held):
            bit, column = b // sz.per_bit, (b % sz.per_bit) * sz.block
            product(highs[b][...], lows[b][...], bit, column, sz.block)
            for index in waiting[:share]:
                stream(index)
            waiting = waiting[share:]
        for index in waiting:
            stream(index)

        partial = place_norms(sz, env, step - 1) + jnp.where(bond == 0, norms, 0.0)
        row = jnp.where(bond == 0, bit_row(sz, bits_ref, group, taken), 0.0)
        for side in range(2):
            for pair in range(sz.half):
                out[side, pair, 0:1, sz.chunk :] = partial
                out[side, pair, 1:2, sz.chunk :] = row
        if not last:
            keep[...] = out[core]
            give[...] = out[1 - core]
            fin_keep[...] = jnp.zeros_like(fin_keep)
            fin_give[...] = jnp.zeros_like(fin_give)
        fin_keep[:, 0 : 2 * rows, :] = out[core]
        fin_give[:, 0 : 2 * rows, :] = out[1 - core]

    @pl.when(group != step)
    def _():
        fin_keep[...] = old_keep[...]
        fin_give[...] = old_give[...]


def add_kernel(sz, keep, came, *outs):
    pair = lax.axis_index("bond") // 2
    for t, out in enumerate(outs):
        target = lax.rem(pair + t, sz.half)
        out[...] = keep[target] + came[target]


def norm_kernel(sz, *refs):
    parts, out = refs[:-1], refs[-1]
    bond = lax.axis_index("bond")
    total = parts[0][...]
    for m in parts[1:]:
        total = total + m[...]
    norms = place_norms(sz, total[:, : sz.chunk], lax.axis_index("seg"))
    known = jnp.where(bond == 0, total[0:2, sz.chunk :], 0.0)
    out[0:1, :] = known[0:1] + norms
    out[1:2, :] = known[1:2]


def sum_kernel(left, right, out):
    out[...] = left[...] + right[...]


def final_kernel(sz, order_ref, *refs):
    parts, out = refs[:-1], refs[-1]
    total = parts[0][...]
    for m in parts[1:]:
        total = total + m[...]
    shape = (sz.rows, sz.extra)
    norms = jnp.broadcast_to(total[0:1], shape)
    taken = jnp.broadcast_to(total[1:2], shape)
    lane = lax.broadcasted_iota(jnp.int32, shape, 1)
    row = lax.broadcasted_iota(jnp.int32, shape, 0)
    group = lax.axis_index("seg")
    prefix = jnp.zeros((sz.rows, 1), jnp.int32)
    square = jnp.ones((sz.rows, 1), F32)
    chosen = jnp.zeros((sz.rows, 1), F32)
    for level in range(sz.segs):
        bit = jnp.sum(jnp.where(lane == row + level * sz.rows, taken, 0.0), axis=1, keepdims=True)
        bit = bit.astype(jnp.int32)
        first = 2 * 2**level - 2
        own = first + prefix + bit * 2**level
        other = first + prefix + (1 - bit) * 2**level
        sum_own = jnp.sum(jnp.where(lane == own, norms, 0.0), axis=1, keepdims=True)
        sum_other = jnp.sum(jnp.where(lane == other, norms, 0.0), axis=1, keepdims=True)
        scale = square * sz.right
        mean_own = sum_own / scale + EPSILON
        mean_other = sum_other / scale + EPSILON
        chosen = jnp.where(group == level, mean_own / (mean_own + mean_other), chosen)
        square = square * mean_own
        prefix = prefix + bit * 2**level
    slots = (sz.rows, sz.rows)
    which = lax.broadcasted_iota(jnp.int32, slots, 0) == jnp.broadcast_to(order_ref[...], slots)
    out[...] = jnp.sum(jnp.where(which, chosen, 0.0), axis=0, keepdims=True)


def shape_of(*dims, dtype=F32):
    return jax.ShapeDtypeStruct(dims, dtype)


def params(limit):
    return pltpu.CompilerParams(vmem_limit_bytes=limit)


def on_device(sites, boundary, bits, order):
    sz = Sizes(sites, bits)
    site = sites.reshape(sites.shape[1:])
    bits = bits.reshape(1, sz.rows)
    half, bonds = sz.half, sz.bonds

    def swap_cores(x, segs):
        return lax.ppermute(x, AXES, [(k * bonds + j, k * bonds + (j ^ 1)) for k in segs for j in range(bonds)])

    def to_pair(x, t, segs, ahead):
        pairs = [
            (k * bonds + j, (k + ahead) * bonds + ((j // 2 + t) % half) * 2 + j % 2)
            for k in segs
            for j in range(bonds)
        ]
        return lax.ppermute(x, AXES, pairs)

    def add(keep, came):
        rows = keep.shape[1]
        return pl.pallas_call(
            functools.partial(add_kernel, sz),
            out_shape=tuple(shape_of(rows, sz.width) for _ in range(half)),
            in_specs=[VMEM, VMEM],
            out_specs=(VMEM,) * half,
            compiler_params=params(MIB),
            name="add_pair",
        )(keep, came)

    part = (sz.left, sz.block)
    fins = (shape_of(half, sz.most, sz.width),) * 2
    ring = pltpu.VMEM((RING, sz.left, sz.piece), F32)
    sems = pltpu.SemaphoreType.DMA((RING,))
    outs = pl.pallas_call(
        functools.partial(first_kernel, sz),
        out_shape=(shape_of(half, 2, sz.width),) * 2 + fins + (pltpu.VMEM(part, BF16),) * (2 * sz.held),
        in_specs=[VMEM, VMEM, ANY],
        out_specs=(VMEM,) * (4 + 2 * sz.held),
        scratch_shapes=[
            ring,
            pltpu.VMEM((sz.left, LANES), F32),
            pltpu.VMEM((2, half, 2, sz.width), F32),
            sems,
        ],
        compiler_params=params(SCOPE),
        name="first_site",
    )(bits, boundary.reshape(1, sz.left), site)
    keep, give, *fin = outs[:4]
    held = [pltpu.with_memory_space_constraint(x, pltpu.VMEM) for x in outs[4:]]

    for step in range(1, sz.segs):
        sums = add(keep, swap_cores(give, [step - 1]))
        messages = [to_pair(x, t, [step - 1], 1) for t, x in enumerate(sums)]
        rows = 2**step
        last = step == sz.segs - 1
        shapes = fins if last else (shape_of(half, 2 * rows, sz.width),) * 2 + fins
        given = 2 + half + 2 * sz.held
        outs = pl.pallas_call(
            functools.partial(site_kernel, sz, step),
            out_shape=shapes,
            in_specs=[VMEM, ANY] + [VMEM] * (half + 2 * sz.held + 2),
            out_specs=(VMEM,) * len(shapes),
            input_output_aliases={given: len(shapes) - 2, given + 1: len(shapes) - 1},
            scratch_shapes=[
                ring,
                pltpu.VMEM((max(16, 2 * rows), sz.left), F32),
                pltpu.VMEM((2, half, 2 * rows, sz.width), F32),
                sems,
            ],
            compiler_params=params(SCOPE),
            name="site_" + str(step),
        )(bits, site, *messages, *held, *fin)
        fin = outs[-2:]
        if not last:
            keep, give = outs[:2]

    every = range(sz.segs)
    sums = add(fin[0], swap_cores(fin[1], every))
    parts = [sums[0]] + [to_pair(sums[t], t, every, 0) for t in range(1, half)]
    tail = pl.pallas_call(
        functools.partial(norm_kernel, sz),
        out_shape=shape_of(2, sz.extra),
        in_specs=[VMEM] * half,
        out_specs=VMEM,
        compiler_params=params(2 * MIB),
        name="norms",
    )(*parts)
    tail = pl.pallas_call(
        sum_kernel,
        out_shape=shape_of(2, sz.extra),
        in_specs=[VMEM] * 2,
        out_specs=VMEM,
        compiler_params=params(MIB),
        name="norms_pair",
    )(tail, swap_cores(tail, every))
    parts = [tail] + [to_pair(tail, t, every, 0) for t in range(1, half)]
    probs = pl.pallas_call(
        functools.partial(final_kernel, sz),
        out_shape=shape_of(1, sz.rows),
        in_specs=[VMEM] * (1 + half),
        out_specs=VMEM,
        compiler_params=params(MIB),
        name="probs",
    )(order.reshape(1, sz.rows), *parts)
    return probs.reshape(sz.rows, 1)


def solution(mesh):
    return jax.shard_map(
        on_device,
        mesh=mesh,
        in_specs=(P("seg", None, "bond", None), P("bond"), P(None, "seg"), P()),
        out_specs=P(None, "seg"),
        check_vma=False,
    )
```

```python
import functools

import jax
import jax.numpy as jnp
from jax import lax
from jax.experimental import pallas as pl
from jax.experimental.pallas import tpu as pltpu
from jax.sharding import PartitionSpec as P

EPSILON = 1e-06
AXES = ("seg", "bond")
LANES = 128
MIB = 2**20
BLOCK = 2048
RING = 4
RINGS = (1, 2)
SCOPE = 43 * MIB // 4
F32 = jnp.float32
BF16 = jnp.bfloat16
F8 = jnp.float8_e4m3fn
TOP = 256.0
TINY = 1e-30
VMEM = pl.BlockSpec(memory_space=pltpu.VMEM)
ANY = pl.BlockSpec(memory_space=pl.ANY)


class Sizes:
    def __init__(self, sites, bits):
        assert sites.shape[0] == 1
        self.segs = lax.axis_size("seg")
        self.bonds = lax.axis_size("bond")
        self.half = self.bonds // 2
        self.left, self.right = sites.shape[2], sites.shape[3]
        self.chunk = self.right // self.bonds
        assert self.chunk == self.left and self.bonds % 2 == 0
        self.rows = bits.shape[0]
        self.most = 2**self.segs
        need = max(2 * self.most - 2, self.rows * self.segs)
        self.extra = -(-need // LANES) * LANES
        self.width = self.chunk + self.extra
        self.block = min(BLOCK, self.right)
        self.per_bit = self.right // self.block
        self.held = 2 * self.per_bit
        self.packs = self.held // 2
        self.piece = min(512, self.chunk)
        self.pieces = self.block // self.piece

    def place(self, column):
        owner = column // self.chunk
        return owner // 2, owner % 2


def split(x):
    high = x.astype(BF16)
    return high, x - high.astype(F32)


def piece_copy(sz, site, ring, sems, index):
    per = sz.right // sz.piece
    column = pl.multiple_of((index % per) * sz.piece, sz.piece)
    slot = index % RING
    return pltpu.make_async_copy(
        site.at[index // per, :, pl.ds(column, sz.piece)], ring.at[slot], sems.at[slot]
    )


def bit_row(sz, bits_ref, group, extra):
    mine = bits_ref[...].astype(F32)
    wide = jnp.concatenate([mine] * (sz.extra // sz.rows), axis=1) if sz.extra > sz.rows else mine
    lane = lax.broadcasted_iota(jnp.int32, (1, sz.extra), 1)
    return extra + jnp.where(lane // sz.rows == group, wide, 0.0)


def first_kernel(
    sz, bits_ref, order_ref, start_ref, site, keep, give, fin_keep, fin_give, bits_out, order_out, scales, *rest
):
    bits_out[...] = bits_ref[...]
    order_out[...] = order_ref[...]
    highs, lows = rest[: sz.held], rest[sz.held : sz.held + sz.packs]
    ring, spread, out, sems = rest[sz.held + sz.packs :]
    group = lax.axis_index("seg")
    bond = lax.axis_index("bond")
    core = bond % 2
    copy = functools.partial(piece_copy, sz, site, ring, sems)

    @pl.when(group == 0)
    def _():
        total = 2 * sz.right // sz.piece
        for i in range(RING):
            copy(i).start()
        turned = jnp.transpose(jnp.broadcast_to(start_ref[...], (8, sz.left)))
        spread[...] = jnp.broadcast_to(turned[:, 0:1], (sz.left, LANES))
        out[...] = jnp.zeros_like(out)
        per = sz.right // sz.piece
        for bit in range(2):

            def body(i, _):
                index = bit * per + i
                slot = index % RING
                copy(index).wait()
                sums = [None] * (sz.piece // LANES)
                for g in range(sz.left // 8):
                    env = spread[g * 8 : (g + 1) * 8, :]
                    for j in range(len(sums)):
                        term = ring[slot, g * 8 : (g + 1) * 8, j * LANES : (j + 1) * LANES] * env
                        sums[j] = term if g == 0 else sums[j] + term

                @pl.when(index + RING < total)
                def _():
                    copy(index + RING).start()

                column = i * sz.piece
                pair, side = sz.place(column)
                offset = pl.multiple_of(column % sz.chunk, sz.piece)
                row = jnp.concatenate([jnp.sum(s, axis=0, keepdims=True) for s in sums], axis=1)
                out[side, pair, bit : bit + 1, pl.ds(offset, sz.piece)] = row
                return 0

            lax.fori_loop(0, per, body, 0)
        none = jnp.zeros((1, sz.extra), F32)
        row = jnp.where(bond == 0, bit_row(sz, bits_ref, group, none), 0.0)
        for side in range(2):
            for pair in range(sz.half):
                out[side, pair, 1:2, sz.chunk :] = row
        keep[...] = out[core]
        give[...] = out[1 - core]
        fin_keep[...] = jnp.zeros_like(fin_keep)
        fin_give[...] = jnp.zeros_like(fin_give)
        fin_keep[:, 0:2, :] = out[core]
        fin_give[:, 0:2, :] = out[1 - core]

    @pl.when(group != 0)
    def _():
        total = sz.held * sz.pieces
        for i in range(min(RING, total)):
            copy(i).start()
        for b in range(sz.held):

            def body(i, _):
                index = b * sz.pieces + i
                slot = index % RING
                copy(index).wait()
                x = ring[slot]
                high, low = split(x)
                column = pl.multiple_of(i * sz.piece, sz.piece)
                highs[b][:, pl.ds(column, sz.piece)] = high
                most = jnp.max(jnp.max(jnp.abs(x), axis=0, keepdims=True), axis=1, keepdims=True)
                most = jnp.maximum(most, TINY)
                column = pl.multiple_of(b % 2 * sz.block + i * sz.piece, sz.piece)
                lows[b // 2][:, pl.ds(column, sz.piece)] = (low * (TOP * TOP / most)).astype(F8)
                scales[pl.ds(index, 1), :] = jnp.broadcast_to(most / (TOP * TOP), (1, LANES))

                @pl.when(index + RING < total)
                def _():
                    copy(index + RING).start()

                return 0

            lax.fori_loop(0, sz.pieces, body, 0)
        keep[...] = jnp.zeros_like(keep)
        give[...] = jnp.zeros_like(give)
        fin_keep[...] = jnp.zeros_like(fin_keep)
        fin_give[...] = jnp.zeros_like(fin_give)


def place_norms(sz, env, level):
    norms = jnp.sum(env * env, axis=1, keepdims=True)
    shape = (env.shape[0], sz.extra)
    lane = lax.broadcasted_iota(jnp.int32, shape, 1)
    row = lax.broadcasted_iota(jnp.int32, shape, 0)
    first = 2 * lax.shift_left(1, level) - 2
    return jnp.sum(jnp.where(lane == row + first, norms, 0.0), axis=0, keepdims=True)


def site_kernel(sz, step, *refs):
    last = step == sz.segs - 1
    refs = list(refs)
    bits_ref, scales = refs[:2]
    messages = refs[2 : 2 + sz.half]
    refs = refs[2 + sz.half :]
    highs, lows = refs[: sz.held], refs[sz.held : sz.held + sz.packs]
    old_keep, old_give = refs[sz.held + sz.packs : sz.held + sz.packs + 2]
    refs = refs[sz.held + sz.packs + 2 :]
    if last:
        fin_keep, fin_give = refs[:2]
        refs = refs[2:]
    else:
        keep, give, fin_keep, fin_give = refs[:4]
        refs = refs[4:]
    lhs_ref, lhs8_ref, out = refs
    group = lax.axis_index("seg")
    bond = lax.axis_index("bond")
    core = bond % 2
    rows = 2**step

    @pl.when(group == step)
    def _():
        total = messages[0][...]
        for m in messages[1:]:
            total = total + m[...]
        env = total[:, : sz.chunk]
        norms = total[0:1, sz.chunk :]
        taken = total[1:2, sz.chunk :]
        high, low = split(env)
        lhs_ref[...] = jnp.zeros_like(lhs_ref)
        lhs_ref[0:rows, :] = high.astype(F32)
        lhs_ref[rows : 2 * rows, :] = low
        lhs = lhs_ref[...].astype(BF16)
        unit = jnp.maximum(jnp.max(jnp.abs(env), axis=1, keepdims=True), TINY) / TOP
        scaled = env / unit
        rough = scaled.astype(F8).astype(F32)
        lhs8_ref[...] = jnp.zeros_like(lhs8_ref)
        lhs8_ref[0:rows, :] = rough
        lhs8_ref[rows : 2 * rows, :] = (scaled - rough) * 16.0
        lhs8 = lhs8_ref[...].astype(F8)
        out[...] = jnp.zeros_like(out)
        size = min(sz.piece, sz.block)
        for b in range(sz.held):
            bit = b // sz.per_bit
            big = jnp.dot(lhs, highs[b][...], preferred_element_type=F32)
            low = lows[b // 2][:, b % 2 * sz.block : (b % 2 + 1) * sz.block]
            small = jnp.dot(lhs8, low, preferred_element_type=F32)
            big = big[0:rows] + big[rows : 2 * rows]
            small = (small[0:rows] + small[rows : 2 * rows] * (1.0 / 16.0)) * unit
            for p in range(sz.pieces):
                column = (b % sz.per_bit) * sz.block + p * size
                pair, side = sz.place(column)
                offset = column % sz.chunk
                cut = slice(p * size, (p + 1) * size)
                index = b * sz.pieces + p
                scale = scales[index : index + 1, 0:1]
                out[side, pair, bit * rows : (bit + 1) * rows, offset : offset + size] = (
                    big[:, cut] + small[:, cut] * scale
                )

        partial = place_norms(sz, env, step - 1) + jnp.where(bond == 0, norms, 0.0)
        row = jnp.where(bond == 0, bit_row(sz, bits_ref, group, taken), 0.0)
        for side in range(2):
            for pair in range(sz.half):
                out[side, pair, 0:1, sz.chunk :] = partial
                out[side, pair, 1:2, sz.chunk :] = row
        if not last:
            keep[...] = out[core]
            give[...] = out[1 - core]
            fin_keep[...] = jnp.zeros_like(fin_keep)
            fin_give[...] = jnp.zeros_like(fin_give)
        fin_keep[:, 0 : 2 * rows, :] = out[core]
        fin_give[:, 0 : 2 * rows, :] = out[1 - core]

    @pl.when(group != step)
    def _():
        fin_keep[...] = old_keep[...]
        fin_give[...] = old_give[...]


def add_kernel(sz, keep, came, *outs):
    pair = lax.axis_index("bond") // 2
    for t, out in enumerate(outs):
        target = lax.rem(pair + t, sz.half)
        out[...] = keep[target] + came[target]


def norm_kernel(sz, *refs):
    parts, out = refs[:-1], refs[-1]
    bond = lax.axis_index("bond")
    total = parts[0][...]
    for m in parts[1:]:
        total = total + m[...]
    norms = place_norms(sz, total[:, : sz.chunk], lax.axis_index("seg"))
    known = jnp.where(bond == 0, total[0:2, sz.chunk :], 0.0)
    out[0:1, :] = known[0:1] + norms
    out[1:2, :] = known[1:2]


def sum_kernel(left, right, out):
    out[...] = left[...] + right[...]


def final_kernel(sz, order_ref, *refs):
    parts, out = refs[:-1], refs[-1]
    total = parts[0][...]
    for m in parts[1:]:
        total = total + m[...]
    shape = (sz.rows, sz.extra)
    norms = jnp.broadcast_to(total[0:1], shape)
    taken = jnp.broadcast_to(total[1:2], shape)
    lane = lax.broadcasted_iota(jnp.int32, shape, 1)
    row = lax.broadcasted_iota(jnp.int32, shape, 0)
    group = lax.axis_index("seg")
    prefix = jnp.zeros((sz.rows, 1), jnp.int32)
    square = jnp.ones((sz.rows, 1), F32)
    chosen = jnp.zeros((sz.rows, 1), F32)
    for level in range(sz.segs):
        bit = jnp.sum(jnp.where(lane == row + level * sz.rows, taken, 0.0), axis=1, keepdims=True)
        bit = bit.astype(jnp.int32)
        first = 2 * 2**level - 2
        own = first + prefix + bit * 2**level
        other = first + prefix + (1 - bit) * 2**level
        sum_own = jnp.sum(jnp.where(lane == own, norms, 0.0), axis=1, keepdims=True)
        sum_other = jnp.sum(jnp.where(lane == other, norms, 0.0), axis=1, keepdims=True)
        scale = square * sz.right
        mean_own = sum_own / scale + EPSILON
        mean_other = sum_other / scale + EPSILON
        chosen = jnp.where(group == level, mean_own / (mean_own + mean_other), chosen)
        square = square * mean_own
        prefix = prefix + bit * 2**level
    slots = (sz.rows, sz.rows)
    which = lax.broadcasted_iota(jnp.int32, slots, 0) == jnp.broadcast_to(order_ref[...], slots)
    out[...] = jnp.sum(jnp.where(which, chosen, 0.0), axis=0, keepdims=True)


def shape_of(*dims, dtype=F32):
    return jax.ShapeDtypeStruct(dims, dtype)


def in_vmem(x):
    return pltpu.with_memory_space_constraint(x, pltpu.VMEM)


def params(limit):
    return pltpu.CompilerParams(vmem_limit_bytes=limit)


def on_device(sites, boundary, bits, order):
    sz = Sizes(sites, bits)
    site = sites.reshape(sites.shape[1:])
    bits = bits.reshape(1, sz.rows)
    half, bonds = sz.half, sz.bonds

    def permute(x, target):
        pairs = [(k * bonds + j, target(k, j)) for k in range(sz.segs) for j in range(bonds)]
        return in_vmem(lax.ppermute(x, AXES, pairs))

    def swap_cores(x):
        return permute(x, lambda k, j: k * bonds + (j ^ 1))

    def to_pair(x, t):
        return permute(x, lambda k, j: k * bonds + (j // 2 + t) % half * 2 + j % 2)

    def hand_over(sums, group):
        alone = [t for t in range(half) if t not in RINGS]
        came = {}
        for t in alone + [t for t in RINGS if t < half]:
            pairs = [
                (k * bonds + j, (k + 1) % sz.segs * bonds + (j // 2 + t) % half * 2 + j % 2)
                for k in ([group] if t in alone else range(sz.segs))
                for j in range(bonds)
            ]
            came[t] = in_vmem(lax.ppermute(sums[t], AXES, pairs))
        return [came[t] for t in range(half)]

    def add(keep, came):
        rows = keep.shape[1]
        return pl.pallas_call(
            functools.partial(add_kernel, sz),
            out_shape=(pltpu.VMEM((rows, sz.width), F32),) * half,
            in_specs=[VMEM, VMEM],
            out_specs=(VMEM,) * half,
            compiler_params=params(MIB),
            name="add_pair",
        )(keep, came)

    part = (sz.left, sz.block)
    fins = (pltpu.VMEM((half, sz.most, sz.width), F32),) * 2
    small = (pltpu.VMEM((1, sz.rows), jnp.int32),) * 2
    ring = pltpu.VMEM((RING, sz.left, sz.piece), F32)
    sems = pltpu.SemaphoreType.DMA((RING,))
    outs = pl.pallas_call(
        functools.partial(first_kernel, sz),
        out_shape=(pltpu.VMEM((half, 2, sz.width), F32),) * 2
        + fins
        + small
        + (pltpu.VMEM((sz.held * sz.pieces, LANES), F32),)
        + (pltpu.VMEM(part, BF16),) * sz.held
        + (pltpu.VMEM((sz.left, 2 * sz.block), F8),) * sz.packs,
        in_specs=[VMEM, VMEM, VMEM, ANY],
        out_specs=(VMEM,) * (7 + sz.held + sz.packs),
        scratch_shapes=[
            ring,
            pltpu.VMEM((sz.left, LANES), F32),
            pltpu.VMEM((2, half, 2, sz.width), F32),
            sems,
        ],
        compiler_params=params(SCOPE),
        name="first_site",
    )(bits, order.reshape(1, sz.rows), boundary.reshape(1, sz.left), site)
    outs = [in_vmem(x) for x in outs]
    keep, give, *fin = outs[:4]
    bits, order, scales = outs[4:7]
    held = outs[7:]

    for step in range(1, sz.segs):
        sums = add(keep, swap_cores(give))
        messages = hand_over(sums, step - 1)
        rows = 2**step
        last = step == sz.segs - 1
        shapes = fins if last else (pltpu.VMEM((half, 2 * rows, sz.width), F32),) * 2 + fins
        given = 2 + half + sz.held + sz.packs
        outs = pl.pallas_call(
            functools.partial(site_kernel, sz, step),
            out_shape=shapes,
            in_specs=[VMEM] * (given + 2),
            out_specs=(VMEM,) * len(shapes),
            input_output_aliases={given: len(shapes) - 2, given + 1: len(shapes) - 1},
            scratch_shapes=[
                pltpu.VMEM((max(16, 2 * rows), sz.left), F32),
                pltpu.VMEM((max(32, 2 * rows), sz.left), F32),
                pltpu.VMEM((2, half, 2 * rows, sz.width), F32),
            ],
            compiler_params=params(SCOPE),
            name="site_" + str(step),
        )(bits, scales, *messages, *held, *fin)
        outs = [in_vmem(x) for x in outs]
        fin = outs[-2:]
        if not last:
            keep, give = outs[:2]

    sums = add(fin[0], swap_cores(fin[1]))
    parts = [in_vmem(sums[0])] + [to_pair(sums[t], t) for t in range(1, half)]
    tail = pl.pallas_call(
        functools.partial(norm_kernel, sz),
        out_shape=pltpu.VMEM((2, sz.extra), F32),
        in_specs=[VMEM] * half,
        out_specs=VMEM,
        compiler_params=params(2 * MIB),
        name="norms",
    )(*parts)
    tail = pl.pallas_call(
        sum_kernel,
        out_shape=pltpu.VMEM((2, sz.extra), F32),
        in_specs=[VMEM] * 2,
        out_specs=VMEM,
        compiler_params=params(MIB),
        name="norms_pair",
    )(in_vmem(tail), swap_cores(tail))
    parts = [in_vmem(tail)] + [to_pair(tail, t) for t in range(1, half)]
    probs = pl.pallas_call(
        functools.partial(final_kernel, sz),
        out_shape=shape_of(1, sz.rows),
        in_specs=[VMEM] * (1 + half),
        out_specs=VMEM,
        compiler_params=params(MIB),
        name="probs",
    )(order, *parts)
    return probs.reshape(sz.rows, 1)


def solution(mesh):
    return jax.shard_map(
        on_device,
        mesh=mesh,
        in_specs=(P("seg", None, "bond", None), P("bond"), P(None, "seg"), P()),
        out_specs=P(None, "seg"),
        check_vma=False,
    )
```

```python
import functools

import jax
import jax.numpy as jnp
from jax import lax
from jax.experimental import pallas as pl
from jax.experimental.pallas import tpu as pltpu
from jax.sharding import PartitionSpec as P

EPSILON = 1e-06
AXES = ("seg", "bond")
LANES = 128
MIB = 2**20
BLOCK = 2048
RING = 4
RINGS = (3, 2)
SCOPE = 43 * MIB // 4
F32 = jnp.float32
BF16 = jnp.bfloat16
F8 = jnp.float8_e4m3fn
TOP = 256.0
TINY = 1e-30
STRIP = 64
VMEM = pl.BlockSpec(memory_space=pltpu.VMEM)
ANY = pl.BlockSpec(memory_space=pl.ANY)


class Sizes:
    def __init__(self, sites, bits):
        assert sites.shape[0] == 1
        self.segs = lax.axis_size("seg")
        self.bonds = lax.axis_size("bond")
        self.half = self.bonds // 2
        near = [t for t in reversed(range(self.half)) if t not in RINGS]
        self.turns = [t for t in RINGS if t < self.half] + near
        self.left, self.right = sites.shape[2], sites.shape[3]
        self.chunk = self.right // self.bonds
        assert self.chunk == self.left and self.bonds % 2 == 0
        self.rows = bits.shape[0]
        self.most = 2**self.segs
        need = max(2 * self.most - 2, self.rows * self.segs)
        self.extra = -(-need // LANES) * LANES
        self.width = self.chunk + self.extra
        self.block = min(BLOCK, self.right)
        self.per_bit = self.right // self.block
        self.held = 2 * self.per_bit
        self.packs = self.held // 2
        self.piece = min(512, self.chunk)
        self.pieces = self.block // self.piece

    def place(self, column):
        owner = column // self.chunk
        return owner // 2, owner % 2


def split(x):
    high = x.astype(BF16)
    return high, x - high.astype(F32)


def piece_copy(sz, site, ring, sems, index):
    per = sz.right // sz.piece
    column = pl.multiple_of((index % per) * sz.piece, sz.piece)
    slot = index % RING
    return pltpu.make_async_copy(
        site.at[index // per, :, pl.ds(column, sz.piece)], ring.at[slot], sems.at[slot]
    )


def bit_row(sz, bits_ref, group, extra):
    mine = bits_ref[...].astype(F32)
    wide = jnp.concatenate([mine] * (sz.extra // sz.rows), axis=1) if sz.extra > sz.rows else mine
    lane = lax.broadcasted_iota(jnp.int32, (1, sz.extra), 1)
    return extra + jnp.where(lane // sz.rows == group, wide, 0.0)


def first_kernel(
    sz, bits_ref, order_ref, start_ref, site, keep, give, fin_keep, fin_give, bits_out, order_out, scales, *rest
):
    bits_out[...] = bits_ref[...]
    order_out[...] = order_ref[...]
    highs, lows = rest[: sz.held], rest[sz.held : sz.held + sz.packs]
    ring, spread, out, sems = rest[sz.held + sz.packs :]
    group = lax.axis_index("seg")
    bond = lax.axis_index("bond")
    core = bond % 2
    copy = functools.partial(piece_copy, sz, site, ring, sems)

    @pl.when(group == 0)
    def _():
        total = 2 * sz.right // sz.piece
        for i in range(RING):
            copy(i).start()
        turned = jnp.transpose(jnp.broadcast_to(start_ref[...], (8, sz.left)))
        spread[...] = jnp.broadcast_to(turned[:, 0:1], (sz.left, LANES))
        out[...] = jnp.zeros_like(out)
        per = sz.right // sz.piece
        for bit in range(2):

            def body(i, _):
                index = bit * per + i
                slot = index % RING
                copy(index).wait()
                sums = [None] * (sz.piece // LANES)
                for g in range(sz.left // 8):
                    env = spread[g * 8 : (g + 1) * 8, :]
                    for j in range(len(sums)):
                        term = ring[slot, g * 8 : (g + 1) * 8, j * LANES : (j + 1) * LANES] * env
                        sums[j] = term if g == 0 else sums[j] + term

                @pl.when(index + RING < total)
                def _():
                    copy(index + RING).start()

                column = i * sz.piece
                pair, side = sz.place(column)
                offset = pl.multiple_of(column % sz.chunk, sz.piece)
                row = jnp.concatenate([jnp.sum(s, axis=0, keepdims=True) for s in sums], axis=1)
                out[side, pair, bit : bit + 1, pl.ds(offset, sz.piece)] = row
                return 0

            lax.fori_loop(0, per, body, 0)
        none = jnp.zeros((1, sz.extra), F32)
        row = jnp.where(bond == 0, bit_row(sz, bits_ref, group, none), 0.0)
        for side in range(2):
            for pair in range(sz.half):
                out[side, pair, 1:2, sz.chunk :] = row
        keep[...] = out[core]
        give[...] = out[1 - core]
        fin_keep[...] = jnp.zeros_like(fin_keep)
        fin_give[...] = jnp.zeros_like(fin_give)
        fin_keep[:, 0:2, :] = out[core]
        fin_give[:, 0:2, :] = out[1 - core]

    @pl.when(group != 0)
    def _():
        total = sz.held * sz.pieces
        for i in range(min(RING, total)):
            copy(i).start()
        for b in range(sz.held):

            def body(i, _):
                index = b * sz.pieces + i
                slot = index % RING
                copy(index).wait()
                strips = [slice(r, r + STRIP) for r in range(0, sz.left, STRIP)]
                most = jnp.abs(ring[slot, strips[0], :])
                for strip in strips[1:]:
                    most = jnp.maximum(most, jnp.abs(ring[slot, strip, :]))
                most = jnp.max(jnp.max(most, axis=0, keepdims=True), axis=1, keepdims=True)
                most = jnp.maximum(most, TINY)
                grow = TOP * TOP / most
                column = pl.multiple_of(i * sz.piece, sz.piece)
                packed = pl.multiple_of(b % 2 * sz.block + i * sz.piece, sz.piece)
                for strip in strips:
                    high, low = split(ring[slot, strip, :])
                    highs[b][strip, pl.ds(column, sz.piece)] = high
                    lows[b // 2][strip, pl.ds(packed, sz.piece)] = (low * grow).astype(F8)
                scales[pl.ds(index, 1), :] = jnp.broadcast_to(most / (TOP * TOP), (1, LANES))

                @pl.when(index + RING < total)
                def _():
                    copy(index + RING).start()

                return 0

            lax.fori_loop(0, sz.pieces, body, 0)
        keep[...] = jnp.zeros_like(keep)
        give[...] = jnp.zeros_like(give)
        fin_keep[...] = jnp.zeros_like(fin_keep)
        fin_give[...] = jnp.zeros_like(fin_give)


def place_norms(sz, env, level):
    norms = jnp.sum(env * env, axis=1, keepdims=True)
    shape = (env.shape[0], sz.extra)
    lane = lax.broadcasted_iota(jnp.int32, shape, 1)
    row = lax.broadcasted_iota(jnp.int32, shape, 0)
    first = 2 * lax.shift_left(1, level) - 2
    return jnp.sum(jnp.where(lane == row + first, norms, 0.0), axis=0, keepdims=True)


def site_kernel(sz, step, *refs):
    last = step == sz.segs - 1
    refs = list(refs)
    bits_ref, scales = refs[:2]
    messages = refs[2 : 2 + sz.half]
    refs = refs[2 + sz.half :]
    highs, lows = refs[: sz.held], refs[sz.held : sz.held + sz.packs]
    old_keep, old_give = refs[sz.held + sz.packs : sz.held + sz.packs + 2]
    refs = refs[sz.held + sz.packs + 2 :]
    if last:
        fin_keep, fin_give = refs[:2]
        refs = refs[2:]
    else:
        keep, give, fin_keep, fin_give = refs[:4]
        refs = refs[4:]
    lhs_ref, lhs8_ref, out = refs
    group = lax.axis_index("seg")
    bond = lax.axis_index("bond")
    core = bond % 2
    rows = 2**step

    @pl.when(group == step)
    def _():
        total = messages[0][...]
        for m in messages[1:]:
            total = total + m[...]
        env = total[:, : sz.chunk]
        norms = total[0:1, sz.chunk :]
        taken = total[1:2, sz.chunk :]
        high, low = split(env)
        lhs_ref[...] = jnp.zeros_like(lhs_ref)
        lhs_ref[0:rows, :] = high.astype(F32)
        lhs_ref[rows : 2 * rows, :] = low
        lhs = lhs_ref[...].astype(BF16)
        unit = jnp.maximum(jnp.max(jnp.abs(env), axis=1, keepdims=True), TINY) / TOP
        scaled = env / unit
        rough = scaled.astype(F8).astype(F32)
        lhs8_ref[...] = jnp.zeros_like(lhs8_ref)
        lhs8_ref[0:rows, :] = rough
        lhs8_ref[rows : 2 * rows, :] = (scaled - rough) * 16.0
        lhs8 = lhs8_ref[...].astype(F8)
        out[...] = jnp.zeros_like(out)
        size = min(sz.piece, sz.block)
        for b in range(sz.held):
            bit = b // sz.per_bit
            big = jnp.dot(lhs, highs[b][...], preferred_element_type=F32)
            low = lows[b // 2][:, b % 2 * sz.block : (b % 2 + 1) * sz.block]
            small = jnp.dot(lhs8, low, preferred_element_type=F32)
            big = big[0:rows] + big[rows : 2 * rows]
            small = (small[0:rows] + small[rows : 2 * rows] * (1.0 / 16.0)) * unit
            for p in range(sz.pieces):
                column = (b % sz.per_bit) * sz.block + p * size
                pair, side = sz.place(column)
                offset = column % sz.chunk
                cut = slice(p * size, (p + 1) * size)
                index = b * sz.pieces + p
                scale = scales[index : index + 1, 0:1]
                out[side, pair, bit * rows : (bit + 1) * rows, offset : offset + size] = (
                    big[:, cut] + small[:, cut] * scale
                )

        partial = place_norms(sz, env, step - 1) + jnp.where(bond == 0, norms, 0.0)
        row = jnp.where(bond == 0, bit_row(sz, bits_ref, group, taken), 0.0)
        for side in range(2):
            for pair in range(sz.half):
                out[side, pair, 0:1, sz.chunk :] = partial
                out[side, pair, 1:2, sz.chunk :] = row
        if not last:
            keep[...] = out[core]
            give[...] = out[1 - core]
            fin_keep[...] = jnp.zeros_like(fin_keep)
            fin_give[...] = jnp.zeros_like(fin_give)
        fin_keep[:, 0 : 2 * rows, :] = out[core]
        fin_give[:, 0 : 2 * rows, :] = out[1 - core]

    @pl.when(group != step)
    def _():
        fin_keep[...] = old_keep[...]
        fin_give[...] = old_give[...]


def add_kernel(sz, keep, came, *outs):
    pair = lax.axis_index("bond") // 2
    for t, out in zip(sz.turns, outs):
        target = lax.rem(pair + t, sz.half)
        out[...] = keep[target] + came[target]


def norm_kernel(sz, *refs):
    parts, out = refs[:-1], refs[-1]
    bond = lax.axis_index("bond")
    total = parts[0][...]
    for m in parts[1:]:
        total = total + m[...]
    norms = place_norms(sz, total[:, : sz.chunk], lax.axis_index("seg"))
    known = jnp.where(bond == 0, total[0:2, sz.chunk :], 0.0)
    out[0:1, :] = known[0:1] + norms
    out[1:2, :] = known[1:2]


def sum_kernel(left, right, out):
    out[...] = left[...] + right[...]


def final_kernel(sz, order_ref, *refs):
    parts, out = refs[:-1], refs[-1]
    total = parts[0][...]
    for m in parts[1:]:
        total = total + m[...]
    shape = (sz.rows, sz.extra)
    norms = jnp.broadcast_to(total[0:1], shape)
    taken = jnp.broadcast_to(total[1:2], shape)
    lane = lax.broadcasted_iota(jnp.int32, shape, 1)
    row = lax.broadcasted_iota(jnp.int32, shape, 0)
    group = lax.axis_index("seg")
    prefix = jnp.zeros((sz.rows, 1), jnp.int32)
    square = jnp.ones((sz.rows, 1), F32)
    chosen = jnp.zeros((sz.rows, 1), F32)
    for level in range(sz.segs):
        bit = jnp.sum(jnp.where(lane == row + level * sz.rows, taken, 0.0), axis=1, keepdims=True)
        bit = bit.astype(jnp.int32)
        first = 2 * 2**level - 2
        own = first + prefix + bit * 2**level
        other = first + prefix + (1 - bit) * 2**level
        sum_own = jnp.sum(jnp.where(lane == own, norms, 0.0), axis=1, keepdims=True)
        sum_other = jnp.sum(jnp.where(lane == other, norms, 0.0), axis=1, keepdims=True)
        scale = square * sz.right
        mean_own = sum_own / scale + EPSILON
        mean_other = sum_other / scale + EPSILON
        chosen = jnp.where(group == level, mean_own / (mean_own + mean_other), chosen)
        square = square * mean_own
        prefix = prefix + bit * 2**level
    slots = (sz.rows, sz.rows)
    which = lax.broadcasted_iota(jnp.int32, slots, 0) == jnp.broadcast_to(order_ref[...], slots)
    out[...] = jnp.sum(jnp.where(which, chosen, 0.0), axis=0, keepdims=True)


def shape_of(*dims, dtype=F32):
    return jax.ShapeDtypeStruct(dims, dtype)


def in_vmem(x):
    return pltpu.with_memory_space_constraint(x, pltpu.VMEM)


def params(limit):
    return pltpu.CompilerParams(vmem_limit_bytes=limit)


def on_device(sites, boundary, bits, order):
    sz = Sizes(sites, bits)
    site = sites.reshape(sites.shape[1:])
    bits = bits.reshape(1, sz.rows)
    half, bonds = sz.half, sz.bonds

    def permute(x, target):
        pairs = [(k * bonds + j, target(k, j)) for k in range(sz.segs) for j in range(bonds)]
        return in_vmem(lax.ppermute(x, AXES, pairs))

    def swap_cores(x):
        return permute(x, lambda k, j: k * bonds + (j ^ 1))

    def to_pair(x, t):
        return permute(x, lambda k, j: k * bonds + (j // 2 + t) % half * 2 + j % 2)

    def hand_over(sums, group):
        came = []
        for t, x in zip(sz.turns, sums):
            pairs = [
                (k * bonds + j, (k + 1) % sz.segs * bonds + (j // 2 + t) % half * 2 + j % 2)
                for k in (range(sz.segs) if t in RINGS and group > 0 else [group])
                for j in range(bonds)
            ]
            came.append(in_vmem(lax.ppermute(x, AXES, pairs)))
        return came

    def add(keep, came):
        rows = keep.shape[1]
        return pl.pallas_call(
            functools.partial(add_kernel, sz),
            out_shape=(pltpu.VMEM((rows, sz.width), F32),) * half,
            in_specs=[VMEM, VMEM],
            out_specs=(VMEM,) * half,
            compiler_params=params(MIB),
            name="add_pair",
        )(keep, came)

    part = (sz.left, sz.block)
    fins = (pltpu.VMEM((half, sz.most, sz.width), F32),) * 2
    small = (pltpu.VMEM((1, sz.rows), jnp.int32),) * 2
    ring = pltpu.VMEM((RING, sz.left, sz.piece), F32)
    sems = pltpu.SemaphoreType.DMA((RING,))
    outs = pl.pallas_call(
        functools.partial(first_kernel, sz),
        out_shape=(pltpu.VMEM((half, 2, sz.width), F32),) * 2
        + fins
        + small
        + (pltpu.VMEM((sz.held * sz.pieces, LANES), F32),)
        + (pltpu.VMEM(part, BF16),) * sz.held
        + (pltpu.VMEM((sz.left, 2 * sz.block), F8),) * sz.packs,
        in_specs=[VMEM, VMEM, VMEM, ANY],
        out_specs=(VMEM,) * (7 + sz.held + sz.packs),
        scratch_shapes=[
            ring,
            pltpu.VMEM((sz.left, LANES), F32),
            pltpu.VMEM((2, half, 2, sz.width), F32),
            sems,
        ],
        compiler_params=params(SCOPE),
        name="first_site",
    )(bits, order.reshape(1, sz.rows), boundary.reshape(1, sz.left), site)
    outs = [in_vmem(x) for x in outs]
    keep, give, *fin = outs[:4]
    bits, order, scales = outs[4:7]
    held = outs[7:]

    for step in range(1, sz.segs):
        sums = add(keep, swap_cores(give))
        messages = hand_over(sums, step - 1)
        rows = 2**step
        last = step == sz.segs - 1
        shapes = fins if last else (pltpu.VMEM((half, 2 * rows, sz.width), F32),) * 2 + fins
        given = 2 + half + sz.held + sz.packs
        outs = pl.pallas_call(
            functools.partial(site_kernel, sz, step),
            out_shape=shapes,
            in_specs=[VMEM] * (given + 2),
            out_specs=(VMEM,) * len(shapes),
            input_output_aliases={given: len(shapes) - 2, given + 1: len(shapes) - 1},
            scratch_shapes=[
                pltpu.VMEM((max(16, 2 * rows), sz.left), F32),
                pltpu.VMEM((max(32, 2 * rows), sz.left), F32),
                pltpu.VMEM((2, half, 2 * rows, sz.width), F32),
            ],
            compiler_params=params(SCOPE),
            name="site_" + str(step),
        )(bits, scales, *messages, *held, *fin)
        outs = [in_vmem(x) for x in outs]
        fin = outs[-2:]
        if not last:
            keep, give = outs[:2]

    sums = add(fin[0], swap_cores(fin[1]))
    parts = [to_pair(x, t) if t else in_vmem(x) for t, x in zip(sz.turns, sums)]
    tail = pl.pallas_call(
        functools.partial(norm_kernel, sz),
        out_shape=pltpu.VMEM((2, sz.extra), F32),
        in_specs=[VMEM] * half,
        out_specs=VMEM,
        compiler_params=params(2 * MIB),
        name="norms",
    )(*parts)
    tail = pl.pallas_call(
        sum_kernel,
        out_shape=pltpu.VMEM((2, sz.extra), F32),
        in_specs=[VMEM] * 2,
        out_specs=VMEM,
        compiler_params=params(MIB),
        name="norms_pair",
    )(in_vmem(tail), swap_cores(tail))
    parts = [in_vmem(tail)] + [to_pair(tail, t) for t in range(1, half)]
    probs = pl.pallas_call(
        functools.partial(final_kernel, sz),
        out_shape=shape_of(1, sz.rows),
        in_specs=[VMEM] * (1 + half),
        out_specs=VMEM,
        compiler_params=params(MIB),
        name="probs",
    )(order, *parts)
    return probs.reshape(sz.rows, 1)


def solution(mesh):
    return jax.shard_map(
        on_device,
        mesh=mesh,
        in_specs=(P("seg", None, "bond", None), P("bond"), P(None, "seg"), P()),
        out_specs=P(None, "seg"),
        check_vma=False,
    )
```

```python
import functools

import jax
import jax.numpy as jnp
from jax import lax
from jax.experimental import pallas as pl
from jax.experimental.pallas import tpu as pltpu
from jax.sharding import PartitionSpec as P

EPSILON = 1e-06
AXES = ("seg", "bond")
LANES = 128
MIB = 2**20
BLOCK = 2048
RING = 4
RINGS = (3, 2)
INNER = (1, 3, 2)
SCOPE = 43 * MIB // 4
F32 = jnp.float32
BF16 = jnp.bfloat16
F8 = jnp.float8_e4m3fn
TOP = 256.0
TINY = 1e-30
STRIP = 64
VMEM = pl.BlockSpec(memory_space=pltpu.VMEM)
ANY = pl.BlockSpec(memory_space=pl.ANY)


class Sizes:
    def __init__(self, sites, bits):
        assert sites.shape[0] == 1
        self.segs = lax.axis_size("seg")
        self.bonds = lax.axis_size("bond")
        self.half = self.bonds // 2
        near = [t for t in reversed(range(self.half)) if t not in RINGS]
        self.turns = [t for t in RINGS if t < self.half] + near
        assert self.half & (self.half - 1) == 0
        self.inner = sorted(range(1, self.half), key=lambda m: INNER.index(m) if m in INNER else -1)
        self.left, self.right = sites.shape[2], sites.shape[3]
        self.chunk = self.right // self.bonds
        assert self.chunk == self.left and self.bonds % 2 == 0
        self.rows = bits.shape[0]
        self.most = 2**self.segs
        need = max(2 * self.most - 2, self.rows * self.segs)
        self.extra = -(-need // LANES) * LANES
        self.width = self.chunk + self.extra
        self.block = min(BLOCK, self.right)
        self.per_bit = self.right // self.block
        self.held = 2 * self.per_bit
        self.packs = self.held // 2
        self.piece = min(512, self.chunk)
        self.pieces = self.block // self.piece

    def place(self, column):
        owner = column // self.chunk
        return owner // 2, owner % 2


def split(x):
    high = x.astype(BF16)
    return high, x - high.astype(F32)


def piece_copy(sz, site, ring, sems, index):
    per = sz.right // sz.piece
    column = pl.multiple_of((index % per) * sz.piece, sz.piece)
    slot = index % RING
    return pltpu.make_async_copy(
        site.at[index // per, :, pl.ds(column, sz.piece)], ring.at[slot], sems.at[slot]
    )


def bit_row(sz, bits_ref, group, extra):
    mine = bits_ref[...].astype(F32)
    wide = jnp.concatenate([mine] * (sz.extra // sz.rows), axis=1) if sz.extra > sz.rows else mine
    lane = lax.broadcasted_iota(jnp.int32, (1, sz.extra), 1)
    return extra + jnp.where(lane // sz.rows == group, wide, 0.0)


def first_kernel(
    sz, bits_ref, order_ref, start_ref, site, keep, give, fin_keep, fin_give, bits_out, order_out, scales, *rest
):
    bits_out[...] = bits_ref[...]
    order_out[...] = order_ref[...]
    highs, lows = rest[: sz.held], rest[sz.held : sz.held + sz.packs]
    ring, spread, out, sems = rest[sz.held + sz.packs :]
    group = lax.axis_index("seg")
    bond = lax.axis_index("bond")
    core = bond % 2
    copy = functools.partial(piece_copy, sz, site, ring, sems)

    @pl.when(group == 0)
    def _():
        total = 2 * sz.right // sz.piece
        for i in range(RING):
            copy(i).start()
        turned = jnp.transpose(jnp.broadcast_to(start_ref[...], (8, sz.left)))
        spread[...] = jnp.broadcast_to(turned[:, 0:1], (sz.left, LANES))
        out[...] = jnp.zeros_like(out)
        per = sz.right // sz.piece
        for bit in range(2):

            def body(i, _):
                index = bit * per + i
                slot = index % RING
                copy(index).wait()
                sums = [None] * (sz.piece // LANES)
                for g in range(sz.left // 8):
                    env = spread[g * 8 : (g + 1) * 8, :]
                    for j in range(len(sums)):
                        term = ring[slot, g * 8 : (g + 1) * 8, j * LANES : (j + 1) * LANES] * env
                        sums[j] = term if g == 0 else sums[j] + term

                @pl.when(index + RING < total)
                def _():
                    copy(index + RING).start()

                column = i * sz.piece
                pair, side = sz.place(column)
                offset = pl.multiple_of(column % sz.chunk, sz.piece)
                row = jnp.concatenate([jnp.sum(s, axis=0, keepdims=True) for s in sums], axis=1)
                out[side, pair, bit : bit + 1, pl.ds(offset, sz.piece)] = row
                return 0

            lax.fori_loop(0, per, body, 0)
        none = jnp.zeros((1, sz.extra), F32)
        row = jnp.where(bond == 0, bit_row(sz, bits_ref, group, none), 0.0)
        for side in range(2):
            for pair in range(sz.half):
                out[side, pair, 1:2, sz.chunk :] = row
        keep[...] = out[core]
        give[...] = out[1 - core]
        fin_keep[...] = jnp.zeros_like(fin_keep)
        fin_give[...] = jnp.zeros_like(fin_give)
        fin_keep[:, 0:2, :] = out[core]
        fin_give[:, 0:2, :] = out[1 - core]

    @pl.when(group != 0)
    def _():
        total = sz.held * sz.pieces
        for i in range(min(RING, total)):
            copy(i).start()
        for b in range(sz.held):

            def body(i, _):
                index = b * sz.pieces + i
                slot = index % RING
                copy(index).wait()
                strips = [slice(r, r + STRIP) for r in range(0, sz.left, STRIP)]
                most = jnp.abs(ring[slot, strips[0], :])
                for strip in strips[1:]:
                    most = jnp.maximum(most, jnp.abs(ring[slot, strip, :]))
                most = jnp.max(jnp.max(most, axis=0, keepdims=True), axis=1, keepdims=True)
                most = jnp.maximum(most, TINY)
                grow = TOP * TOP / most
                column = pl.multiple_of(i * sz.piece, sz.piece)
                packed = pl.multiple_of(b % 2 * sz.block + i * sz.piece, sz.piece)
                for strip in strips:
                    high, low = split(ring[slot, strip, :])
                    highs[b][strip, pl.ds(column, sz.piece)] = high
                    lows[b // 2][strip, pl.ds(packed, sz.piece)] = (low * grow).astype(F8)
                scales[pl.ds(index, 1), :] = jnp.broadcast_to(most / (TOP * TOP), (1, LANES))

                @pl.when(index + RING < total)
                def _():
                    copy(index + RING).start()

                return 0

            lax.fori_loop(0, sz.pieces, body, 0)
        keep[...] = jnp.zeros_like(keep)
        give[...] = jnp.zeros_like(give)
        fin_keep[...] = jnp.zeros_like(fin_keep)
        fin_give[...] = jnp.zeros_like(fin_give)


def place_norms(sz, env, level):
    norms = jnp.sum(env * env, axis=1, keepdims=True)
    shape = (env.shape[0], sz.extra)
    lane = lax.broadcasted_iota(jnp.int32, shape, 1)
    row = lax.broadcasted_iota(jnp.int32, shape, 0)
    first = 2 * lax.shift_left(1, level) - 2
    return jnp.sum(jnp.where(lane == row + first, norms, 0.0), axis=0, keepdims=True)


def site_kernel(sz, step, *refs):
    last = step == sz.segs - 1
    refs = list(refs)
    bits_ref, scales = refs[:2]
    messages = refs[2 : 2 + sz.half]
    refs = refs[2 + sz.half :]
    highs, lows = refs[: sz.held], refs[sz.held : sz.held + sz.packs]
    old_keep, old_give = refs[sz.held + sz.packs : sz.held + sz.packs + 2]
    refs = refs[sz.held + sz.packs + 2 :]
    if last:
        fin_keep, fin_give = refs[:2]
        refs = refs[2:]
    else:
        keep, give, fin_keep, fin_give = refs[:4]
        refs = refs[4:]
    lhs_ref, lhs8_ref, out = refs
    group = lax.axis_index("seg")
    bond = lax.axis_index("bond")
    core = bond % 2
    rows = 2**step

    @pl.when(group == step)
    def _():
        total = messages[0][...]
        for m in messages[1:]:
            total = total + m[...]
        env = total[:, : sz.chunk]
        norms = total[0:1, sz.chunk :]
        taken = total[1:2, sz.chunk :]
        high, low = split(env)
        lhs_ref[...] = jnp.zeros_like(lhs_ref)
        lhs_ref[0:rows, :] = high.astype(F32)
        lhs_ref[rows : 2 * rows, :] = low
        lhs = lhs_ref[...].astype(BF16)
        unit = jnp.maximum(jnp.max(jnp.abs(env), axis=1, keepdims=True), TINY) / TOP
        scaled = env / unit
        rough = scaled.astype(F8).astype(F32)
        lhs8_ref[...] = jnp.zeros_like(lhs8_ref)
        lhs8_ref[0:rows, :] = rough
        lhs8_ref[rows : 2 * rows, :] = (scaled - rough) * 16.0
        lhs8 = lhs8_ref[...].astype(F8)
        out[...] = jnp.zeros_like(out)
        size = min(sz.piece, sz.block)
        for b in range(sz.held):
            bit = b // sz.per_bit
            big = jnp.dot(lhs, highs[b][...], preferred_element_type=F32)
            low = lows[b // 2][:, b % 2 * sz.block : (b % 2 + 1) * sz.block]
            small = jnp.dot(lhs8, low, preferred_element_type=F32)
            big = big[0:rows] + big[rows : 2 * rows]
            small = (small[0:rows] + small[rows : 2 * rows] * (1.0 / 16.0)) * unit
            for p in range(sz.pieces):
                column = (b % sz.per_bit) * sz.block + p * size
                pair, side = sz.place(column)
                offset = column % sz.chunk
                cut = slice(p * size, (p + 1) * size)
                index = b * sz.pieces + p
                scale = scales[index : index + 1, 0:1]
                out[side, pair, bit * rows : (bit + 1) * rows, offset : offset + size] = (
                    big[:, cut] + small[:, cut] * scale
                )

        partial = place_norms(sz, env, step - 1) + jnp.where(bond == 0, norms, 0.0)
        row = jnp.where(bond == 0, bit_row(sz, bits_ref, group, taken), 0.0)
        for side in range(2):
            for pair in range(sz.half):
                out[side, pair, 0:1, sz.chunk :] = partial
                out[side, pair, 1:2, sz.chunk :] = row
        if not last:
            keep[...] = out[core]
            give[...] = out[1 - core]
            fin_keep[...] = jnp.zeros_like(fin_keep)
            fin_give[...] = jnp.zeros_like(fin_give)
        fin_keep[:, 0 : 2 * rows, :] = out[core]
        fin_give[:, 0 : 2 * rows, :] = out[1 - core]

    @pl.when(group != step)
    def _():
        fin_keep[...] = old_keep[...]
        fin_give[...] = old_give[...]


def add_kernel(sz, ahead, keep, came, *outs):
    pair = lax.axis_index("bond") // 2
    if ahead:
        targets = [lax.rem(pair + t, sz.half) for t in sz.turns]
    else:
        targets = [lax.bitwise_xor(pair, m) for m in [*sz.inner, 0]]
    for target, out in zip(targets, outs):
        out[...] = keep[target] + came[target]


def norm_kernel(sz, *refs):
    parts, out = refs[:-1], refs[-1]
    bond = lax.axis_index("bond")
    total = parts[0][...]
    for m in parts[1:]:
        total = total + m[...]
    norms = place_norms(sz, total[:, : sz.chunk], lax.axis_index("seg"))
    known = jnp.where(bond == 0, total[0:2, sz.chunk :], 0.0)
    out[0:1, :] = known[0:1] + norms
    out[1:2, :] = known[1:2]


def sum_kernel(left, right, out):
    out[...] = left[...] + right[...]


def final_kernel(sz, order_ref, *refs):
    parts, out = refs[:-1], refs[-1]
    total = parts[0][...]
    for m in parts[1:]:
        total = total + m[...]
    shape = (sz.rows, sz.extra)
    norms = jnp.broadcast_to(total[0:1], shape)
    taken = jnp.broadcast_to(total[1:2], shape)
    lane = lax.broadcasted_iota(jnp.int32, shape, 1)
    row = lax.broadcasted_iota(jnp.int32, shape, 0)
    group = lax.axis_index("seg")
    prefix = jnp.zeros((sz.rows, 1), jnp.int32)
    square = jnp.ones((sz.rows, 1), F32)
    chosen = jnp.zeros((sz.rows, 1), F32)
    for level in range(sz.segs):
        bit = jnp.sum(jnp.where(lane == row + level * sz.rows, taken, 0.0), axis=1, keepdims=True)
        bit = bit.astype(jnp.int32)
        first = 2 * 2**level - 2
        own = first + prefix + bit * 2**level
        other = first + prefix + (1 - bit) * 2**level
        sum_own = jnp.sum(jnp.where(lane == own, norms, 0.0), axis=1, keepdims=True)
        sum_other = jnp.sum(jnp.where(lane == other, norms, 0.0), axis=1, keepdims=True)
        scale = square * sz.right
        mean_own = sum_own / scale + EPSILON
        mean_other = sum_other / scale + EPSILON
        chosen = jnp.where(group == level, mean_own / (mean_own + mean_other), chosen)
        square = square * mean_own
        prefix = prefix + bit * 2**level
    slots = (sz.rows, sz.rows)
    which = lax.broadcasted_iota(jnp.int32, slots, 0) == jnp.broadcast_to(order_ref[...], slots)
    out[...] = jnp.sum(jnp.where(which, chosen, 0.0), axis=0, keepdims=True)


def shape_of(*dims, dtype=F32):
    return jax.ShapeDtypeStruct(dims, dtype)


def in_vmem(x):
    return pltpu.with_memory_space_constraint(x, pltpu.VMEM)


def params(limit):
    return pltpu.CompilerParams(vmem_limit_bytes=limit)


def on_device(sites, boundary, bits, order):
    sz = Sizes(sites, bits)
    site = sites.reshape(sites.shape[1:])
    bits = bits.reshape(1, sz.rows)
    half, bonds = sz.half, sz.bonds

    def permute(x, target):
        pairs = [(k * bonds + j, target(k, j)) for k in range(sz.segs) for j in range(bonds)]
        return in_vmem(lax.ppermute(x, AXES, pairs))

    def swap_cores(x):
        return permute(x, lambda k, j: k * bonds + (j ^ 1))

    def to_pair(x, m):
        return permute(x, lambda k, j: k * bonds + (j // 2 ^ m) * 2 + j % 2)

    def hand_over(sums, group):
        came = []
        for t, x in zip(sz.turns, sums):
            pairs = [
                (k * bonds + j, (k + 1) % sz.segs * bonds + (j // 2 + t) % half * 2 + j % 2)
                for k in (range(sz.segs) if t in RINGS and group > 0 else [group])
                for j in range(bonds)
            ]
            came.append(in_vmem(lax.ppermute(x, AXES, pairs)))
        return came

    def add(keep, came, ahead):
        rows = keep.shape[1]
        return pl.pallas_call(
            functools.partial(add_kernel, sz, ahead),
            out_shape=(pltpu.VMEM((rows, sz.width), F32),) * half,
            in_specs=[VMEM, VMEM],
            out_specs=(VMEM,) * half,
            compiler_params=params(MIB),
            name="add_pair",
        )(keep, came)

    part = (sz.left, sz.block)
    fins = (pltpu.VMEM((half, sz.most, sz.width), F32),) * 2
    small = (pltpu.VMEM((1, sz.rows), jnp.int32),) * 2
    ring = pltpu.VMEM((RING, sz.left, sz.piece), F32)
    sems = pltpu.SemaphoreType.DMA((RING,))
    outs = pl.pallas_call(
        functools.partial(first_kernel, sz),
        out_shape=(pltpu.VMEM((half, 2, sz.width), F32),) * 2
        + fins
        + small
        + (pltpu.VMEM((sz.held * sz.pieces, LANES), F32),)
        + (pltpu.VMEM(part, BF16),) * sz.held
        + (pltpu.VMEM((sz.left, 2 * sz.block), F8),) * sz.packs,
        in_specs=[VMEM, VMEM, VMEM, ANY],
        out_specs=(VMEM,) * (7 + sz.held + sz.packs),
        scratch_shapes=[
            ring,
            pltpu.VMEM((sz.left, LANES), F32),
            pltpu.VMEM((2, half, 2, sz.width), F32),
            sems,
        ],
        compiler_params=params(SCOPE),
        name="first_site",
    )(bits, order.reshape(1, sz.rows), boundary.reshape(1, sz.left), site)
    outs = [in_vmem(x) for x in outs]
    keep, give, *fin = outs[:4]
    bits, order, scales = outs[4:7]
    held = outs[7:]

    for step in range(1, sz.segs):
        sums = add(keep, swap_cores(give), True)
        messages = hand_over(sums, step - 1)
        rows = 2**step
        last = step == sz.segs - 1
        shapes = fins if last else (pltpu.VMEM((half, 2 * rows, sz.width), F32),) * 2 + fins
        given = 2 + half + sz.held + sz.packs
        outs = pl.pallas_call(
            functools.partial(site_kernel, sz, step),
            out_shape=shapes,
            in_specs=[VMEM] * (given + 2),
            out_specs=(VMEM,) * len(shapes),
            input_output_aliases={given: len(shapes) - 2, given + 1: len(shapes) - 1},
            scratch_shapes=[
                pltpu.VMEM((max(16, 2 * rows), sz.left), F32),
                pltpu.VMEM((max(32, 2 * rows), sz.left), F32),
                pltpu.VMEM((2, half, 2 * rows, sz.width), F32),
            ],
            compiler_params=params(SCOPE),
            name="site_" + str(step),
        )(bits, scales, *messages, *held, *fin)
        outs = [in_vmem(x) for x in outs]
        fin = outs[-2:]
        if not last:
            keep, give = outs[:2]

    sums = add(fin[0], swap_cores(fin[1]), False)
    parts = [to_pair(x, m) for m, x in zip(sz.inner, sums)] + [in_vmem(sums[-1])]
    tail = pl.pallas_call(
        functools.partial(norm_kernel, sz),
        out_shape=pltpu.VMEM((2, sz.extra), F32),
        in_specs=[VMEM] * half,
        out_specs=VMEM,
        compiler_params=params(2 * MIB),
        name="norms",
    )(*parts)
    tail = pl.pallas_call(
        sum_kernel,
        out_shape=pltpu.VMEM((2, sz.extra), F32),
        in_specs=[VMEM] * 2,
        out_specs=VMEM,
        compiler_params=params(MIB),
        name="norms_pair",
    )(in_vmem(tail), swap_cores(tail))
    parts = [in_vmem(tail)] + [to_pair(tail, m) for m in sz.inner]
    probs = pl.pallas_call(
        functools.partial(final_kernel, sz),
        out_shape=shape_of(1, sz.rows),
        in_specs=[VMEM] * (1 + half),
        out_specs=VMEM,
        compiler_params=params(MIB),
        name="probs",
    )(order, *parts)
    return probs.reshape(sz.rows, 1)


def solution(mesh):
    return jax.shard_map(
        on_device,
        mesh=mesh,
        in_specs=(P("seg", None, "bond", None), P("bond"), P(None, "seg"), P()),
        out_specs=P(None, "seg"),
        check_vma=False,
    )
```

```python
import functools

import jax
import jax.numpy as jnp
from jax import lax
from jax.experimental import pallas as pl
from jax.experimental.pallas import tpu as pltpu
from jax.sharding import PartitionSpec as P

EPSILON = 1e-06
AXES = ("seg", "bond")
LANES = 128
MIB = 2**20
BLOCK = 2048
RING = 4
RINGS = (3, 2)
INNER = (1, 3, 2)
SCOPE = 43 * MIB // 4
F32 = jnp.float32
BF16 = jnp.bfloat16
F8 = jnp.float8_e4m3fn
TOP = 256.0
TINY = 1e-30
STRIP = 64
VMEM = pl.BlockSpec(memory_space=pltpu.VMEM)
ANY = pl.BlockSpec(memory_space=pl.ANY)


class Sizes:
    def __init__(self, sites, bits):
        assert sites.shape[0] == 1
        self.segs = lax.axis_size("seg")
        self.bonds = lax.axis_size("bond")
        self.half = self.bonds // 2
        near = [t for t in reversed(range(self.half)) if t not in RINGS]
        self.turns = [t for t in RINGS if t < self.half] + near
        assert self.half & (self.half - 1) == 0
        self.inner = sorted(range(1, self.half), key=lambda m: INNER.index(m) if m in INNER else -1)
        self.left, self.right = sites.shape[2], sites.shape[3]
        self.chunk = self.right // self.bonds
        assert self.chunk == self.left and self.bonds % 2 == 0
        self.rows = bits.shape[0]
        self.most = 2**self.segs
        need = max(2 * self.most - 2, self.rows * self.segs)
        self.extra = -(-need // LANES) * LANES
        self.width = self.chunk + self.extra
        self.block = min(BLOCK, self.right)
        self.per_bit = self.right // self.block
        self.held = 2 * self.per_bit
        self.packs = self.held // 2
        self.piece = min(512, self.chunk)
        self.pieces = self.block // self.piece

    def place(self, column):
        owner = column // self.chunk
        return owner // 2, owner % 2


def split(x):
    high = x.astype(BF16)
    return high, x - high.astype(F32)


def piece_copy(sz, site, ring, sems, index):
    per = sz.right // sz.piece
    column = pl.multiple_of((index % per) * sz.piece, sz.piece)
    slot = index % RING
    return pltpu.make_async_copy(
        site.at[index // per, :, pl.ds(column, sz.piece)], ring.at[slot], sems.at[slot]
    )


def bit_row(sz, bits_ref, group, extra):
    mine = bits_ref[...].astype(F32)
    wide = jnp.concatenate([mine] * (sz.extra // sz.rows), axis=1) if sz.extra > sz.rows else mine
    lane = lax.broadcasted_iota(jnp.int32, (1, sz.extra), 1)
    return extra + jnp.where(lane // sz.rows == group, wide, 0.0)


def first_kernel(
    sz, bits_ref, order_ref, start_ref, site, keep, give, fin_keep, fin_give, bits_out, order_out, scales, *rest
):
    bits_out[...] = bits_ref[...]
    order_out[...] = order_ref[...]
    highs, lows = rest[: sz.held], rest[sz.held : sz.held + sz.packs]
    ring, spread, out, sems = rest[sz.held + sz.packs :]
    group = lax.axis_index("seg")
    bond = lax.axis_index("bond")
    core = bond % 2
    copy = functools.partial(piece_copy, sz, site, ring, sems)

    @pl.when(group == 0)
    def _():
        total = 2 * sz.right // sz.piece
        for i in range(RING):
            copy(i).start()
        turned = jnp.transpose(jnp.broadcast_to(start_ref[...], (8, sz.left)))
        spread[...] = jnp.broadcast_to(turned[:, 0:1], (sz.left, LANES))
        out[...] = jnp.zeros_like(out)
        per = sz.right // sz.piece
        for bit in range(2):

            def body(i, _):
                index = bit * per + i
                slot = index % RING
                copy(index).wait()
                sums = [None] * (sz.piece // LANES)
                for g in range(sz.left // 8):
                    env = spread[g * 8 : (g + 1) * 8, :]
                    for j in range(len(sums)):
                        term = ring[slot, g * 8 : (g + 1) * 8, j * LANES : (j + 1) * LANES] * env
                        sums[j] = term if g == 0 else sums[j] + term

                @pl.when(index + RING < total)
                def _():
                    copy(index + RING).start()

                column = i * sz.piece
                pair, side = sz.place(column)
                offset = pl.multiple_of(column % sz.chunk, sz.piece)
                row = jnp.concatenate([jnp.sum(s, axis=0, keepdims=True) for s in sums], axis=1)
                out[side, pair, bit : bit + 1, pl.ds(offset, sz.piece)] = row
                return 0

            lax.fori_loop(0, per, body, 0)
        none = jnp.zeros((1, sz.extra), F32)
        row = jnp.where(bond == 0, bit_row(sz, bits_ref, group, none), 0.0)
        for side in range(2):
            for pair in range(sz.half):
                out[side, pair, 1:2, sz.chunk :] = row
        keep[...] = out[core]
        give[...] = out[1 - core]
        fin_keep[...] = jnp.zeros_like(fin_keep)
        fin_give[...] = jnp.zeros_like(fin_give)
        fin_keep[:, 0:2, :] = out[core]
        fin_give[:, 0:2, :] = out[1 - core]

    @pl.when(group != 0)
    def _():
        total = sz.held * sz.pieces
        for i in range(min(RING, total)):
            copy(i).start()
        for b in range(sz.held):

            def body(i, _):
                index = b * sz.pieces + i
                slot = index % RING
                copy(index).wait()
                strips = [slice(r, r + STRIP) for r in range(0, sz.left, STRIP)]
                most = jnp.abs(ring[slot, strips[0], :])
                for strip in strips[1:]:
                    most = jnp.maximum(most, jnp.abs(ring[slot, strip, :]))
                most = jnp.max(jnp.max(most, axis=0, keepdims=True), axis=1, keepdims=True)
                most = jnp.maximum(most, TINY)
                grow = TOP * TOP / most
                column = pl.multiple_of(i * sz.piece, sz.piece)
                packed = pl.multiple_of(b % 2 * sz.block + i * sz.piece, sz.piece)
                for strip in strips:
                    high, low = split(ring[slot, strip, :])
                    highs[b][strip, pl.ds(column, sz.piece)] = high
                    lows[b // 2][strip, pl.ds(packed, sz.piece)] = (low * grow).astype(F8)
                scales[pl.ds(index, 1), :] = jnp.broadcast_to(most / (TOP * TOP), (1, LANES))

                @pl.when(index + RING < total)
                def _():
                    copy(index + RING).start()

                return 0

            lax.fori_loop(0, sz.pieces, body, 0)
        keep[...] = jnp.zeros_like(keep)
        give[...] = jnp.zeros_like(give)
        fin_keep[...] = jnp.zeros_like(fin_keep)
        fin_give[...] = jnp.zeros_like(fin_give)


def place_norms(sz, env, level):
    norms = jnp.sum(env * env, axis=1, keepdims=True)
    shape = (env.shape[0], sz.extra)
    lane = lax.broadcasted_iota(jnp.int32, shape, 1)
    row = lax.broadcasted_iota(jnp.int32, shape, 0)
    first = 2 * lax.shift_left(1, level) - 2
    return jnp.sum(jnp.where(lane == row + first, norms, 0.0), axis=0, keepdims=True)


def site_kernel(sz, step, *refs):
    last = step == sz.segs - 1
    refs = list(refs)
    bits_ref, scales = refs[:2]
    messages = refs[2 : 2 + sz.half]
    refs = refs[2 + sz.half :]
    highs, lows = refs[: sz.held], refs[sz.held : sz.held + sz.packs]
    old_keep, old_give = refs[sz.held + sz.packs : sz.held + sz.packs + 2]
    refs = refs[sz.held + sz.packs + 2 :]
    if last:
        fin_keep, fin_give = refs[:2]
        refs = refs[2:]
    else:
        keep, give, fin_keep, fin_give = refs[:4]
        refs = refs[4:]
    lhs_ref, lhs8_ref, out = refs
    group = lax.axis_index("seg")
    bond = lax.axis_index("bond")
    core = bond % 2
    rows = 2**step

    @pl.when(group == step)
    def _():
        total = messages[0][...]
        for m in messages[1:]:
            total = total + m[...]
        env = total[:, : sz.chunk]
        norms = total[0:1, sz.chunk :]
        taken = total[1:2, sz.chunk :]
        high, low = split(env)
        lhs_ref[...] = jnp.zeros_like(lhs_ref)
        lhs_ref[0:rows, :] = high.astype(F32)
        lhs_ref[rows : 2 * rows, :] = low
        lhs = lhs_ref[...].astype(BF16)
        unit = jnp.maximum(jnp.max(jnp.abs(env), axis=1, keepdims=True), TINY) / TOP
        scaled = env / unit
        rough = scaled.astype(F8).astype(F32)
        lhs8_ref[...] = jnp.zeros_like(lhs8_ref)
        lhs8_ref[0:rows, :] = rough
        lhs8_ref[rows : 2 * rows, :] = (scaled - rough) * 16.0
        lhs8 = lhs8_ref[...].astype(F8)
        out[:, :, :, sz.chunk :] = jnp.zeros((2, sz.half, 2 * rows, sz.extra), F32)
        size = min(sz.piece, sz.block)
        for b in range(sz.held):
            bit = b // sz.per_bit
            big = jnp.dot(lhs, highs[b][...], preferred_element_type=F32)
            low = lows[b // 2][:, b % 2 * sz.block : (b % 2 + 1) * sz.block]
            small = jnp.dot(lhs8, low, preferred_element_type=F32)
            big = big[0:rows] + big[rows : 2 * rows]
            small = (small[0:rows] + small[rows : 2 * rows] * (1.0 / 16.0)) * unit
            for p in range(sz.pieces):
                column = (b % sz.per_bit) * sz.block + p * size
                pair, side = sz.place(column)
                offset = column % sz.chunk
                cut = slice(p * size, (p + 1) * size)
                index = b * sz.pieces + p
                scale = scales[index : index + 1, 0:1]
                out[side, pair, bit * rows : (bit + 1) * rows, offset : offset + size] = (
                    big[:, cut] + small[:, cut] * scale
                )

        partial = place_norms(sz, env, step - 1) + jnp.where(bond == 0, norms, 0.0)
        row = jnp.where(bond == 0, bit_row(sz, bits_ref, group, taken), 0.0)
        for side in range(2):
            for pair in range(sz.half):
                out[side, pair, 0:1, sz.chunk :] = partial
                out[side, pair, 1:2, sz.chunk :] = row
        if not last:
            keep[...] = out[core]
            give[...] = out[1 - core]
            fin_keep[...] = jnp.zeros_like(fin_keep)
            fin_give[...] = jnp.zeros_like(fin_give)
        fin_keep[:, 0 : 2 * rows, :] = out[core]
        fin_give[:, 0 : 2 * rows, :] = out[1 - core]

    @pl.when(group != step)
    def _():
        fin_keep[...] = old_keep[...]
        fin_give[...] = old_give[...]


def add_kernel(sz, ahead, keep, came, *outs):
    pair = lax.axis_index("bond") // 2
    if ahead:
        targets = [lax.rem(pair + t, sz.half) for t in sz.turns]
    else:
        targets = [lax.bitwise_xor(pair, m) for m in [*sz.inner, 0]]
    for target, out in zip(targets, outs):
        out[...] = keep[target] + came[target]


def norm_kernel(sz, *refs):
    parts, out = refs[:-1], refs[-1]
    bond = lax.axis_index("bond")
    total = parts[0][...]
    for m in parts[1:]:
        total = total + m[...]
    norms = place_norms(sz, total[:, : sz.chunk], lax.axis_index("seg"))
    known = jnp.where(bond == 0, total[0:2, sz.chunk :], 0.0)
    out[0:1, :] = known[0:1] + norms
    out[1:2, :] = known[1:2]


def sum_kernel(left, right, out):
    out[...] = left[...] + right[...]


def final_kernel(sz, order_ref, *refs):
    parts, out = refs[:-1], refs[-1]
    total = parts[0][...]
    for m in parts[1:]:
        total = total + m[...]
    shape = (sz.rows, sz.extra)
    norms = jnp.broadcast_to(total[0:1], shape)
    taken = jnp.broadcast_to(total[1:2], shape)
    lane = lax.broadcasted_iota(jnp.int32, shape, 1)
    row = lax.broadcasted_iota(jnp.int32, shape, 0)
    group = lax.axis_index("seg")
    prefix = jnp.zeros((sz.rows, 1), jnp.int32)
    square = jnp.ones((sz.rows, 1), F32)
    chosen = jnp.zeros((sz.rows, 1), F32)
    for level in range(sz.segs):
        bit = jnp.sum(jnp.where(lane == row + level * sz.rows, taken, 0.0), axis=1, keepdims=True)
        bit = bit.astype(jnp.int32)
        first = 2 * 2**level - 2
        own = first + prefix + bit * 2**level
        other = first + prefix + (1 - bit) * 2**level
        sum_own = jnp.sum(jnp.where(lane == own, norms, 0.0), axis=1, keepdims=True)
        sum_other = jnp.sum(jnp.where(lane == other, norms, 0.0), axis=1, keepdims=True)
        scale = square * sz.right
        mean_own = sum_own / scale + EPSILON
        mean_other = sum_other / scale + EPSILON
        chosen = jnp.where(group == level, mean_own / (mean_own + mean_other), chosen)
        square = square * mean_own
        prefix = prefix + bit * 2**level
    slots = (sz.rows, sz.rows)
    which = lax.broadcasted_iota(jnp.int32, slots, 0) == jnp.broadcast_to(order_ref[...], slots)
    out[...] = jnp.sum(jnp.where(which, chosen, 0.0), axis=0, keepdims=True)


def shape_of(*dims, dtype=F32):
    return jax.ShapeDtypeStruct(dims, dtype)


def in_vmem(x):
    return pltpu.with_memory_space_constraint(x, pltpu.VMEM)


def params(limit):
    return pltpu.CompilerParams(vmem_limit_bytes=limit)


def on_device(sites, boundary, bits, order):
    sz = Sizes(sites, bits)
    site = sites.reshape(sites.shape[1:])
    bits = bits.reshape(1, sz.rows)
    half, bonds = sz.half, sz.bonds

    def permute(x, target):
        pairs = [(k * bonds + j, target(k, j)) for k in range(sz.segs) for j in range(bonds)]
        return in_vmem(lax.ppermute(x, AXES, pairs))

    def swap_cores(x):
        return permute(x, lambda k, j: k * bonds + (j ^ 1))

    def to_pair(x, m):
        return permute(x, lambda k, j: k * bonds + (j // 2 ^ m) * 2 + j % 2)

    def hand_over(sums, group):
        came = []
        for t, x in zip(sz.turns, sums):
            pairs = [
                (k * bonds + j, (k + 1) % sz.segs * bonds + (j // 2 + t) % half * 2 + j % 2)
                for k in (range(sz.segs) if t in RINGS and group > 0 else [group])
                for j in range(bonds)
            ]
            came.append(in_vmem(lax.ppermute(x, AXES, pairs)))
        return came

    def add(keep, came, ahead):
        rows = keep.shape[1]
        return pl.pallas_call(
            functools.partial(add_kernel, sz, ahead),
            out_shape=(pltpu.VMEM((rows, sz.width), F32),) * half,
            in_specs=[VMEM, VMEM],
            out_specs=(VMEM,) * half,
            compiler_params=params(MIB),
            name="add_pair",
        )(keep, came)

    part = (sz.left, sz.block)
    fins = (pltpu.VMEM((half, sz.most, sz.width), F32),) * 2
    small = (pltpu.VMEM((1, sz.rows), jnp.int32),) * 2
    ring = pltpu.VMEM((RING, sz.left, sz.piece), F32)
    sems = pltpu.SemaphoreType.DMA((RING,))
    outs = pl.pallas_call(
        functools.partial(first_kernel, sz),
        out_shape=(pltpu.VMEM((half, 2, sz.width), F32),) * 2
        + fins
        + small
        + (pltpu.VMEM((sz.held * sz.pieces, LANES), F32),)
        + (pltpu.VMEM(part, BF16),) * sz.held
        + (pltpu.VMEM((sz.left, 2 * sz.block), F8),) * sz.packs,
        in_specs=[VMEM, VMEM, VMEM, ANY],
        out_specs=(VMEM,) * (7 + sz.held + sz.packs),
        scratch_shapes=[
            ring,
            pltpu.VMEM((sz.left, LANES), F32),
            pltpu.VMEM((2, half, 2, sz.width), F32),
            sems,
        ],
        compiler_params=params(SCOPE),
        name="first_site",
    )(bits, order.reshape(1, sz.rows), boundary.reshape(1, sz.left), site)
    outs = [in_vmem(x) for x in outs]
    keep, give, *fin = outs[:4]
    bits, order, scales = outs[4:7]
    held = outs[7:]

    for step in range(1, sz.segs):
        sums = add(keep, swap_cores(give), True)
        messages = hand_over(sums, step - 1)
        rows = 2**step
        last = step == sz.segs - 1
        shapes = fins if last else (pltpu.VMEM((half, 2 * rows, sz.width), F32),) * 2 + fins
        given = 2 + half + sz.held + sz.packs
        outs = pl.pallas_call(
            functools.partial(site_kernel, sz, step),
            out_shape=shapes,
            in_specs=[VMEM] * (given + 2),
            out_specs=(VMEM,) * len(shapes),
            input_output_aliases={given: len(shapes) - 2, given + 1: len(shapes) - 1},
            scratch_shapes=[
                pltpu.VMEM((max(16, 2 * rows), sz.left), F32),
                pltpu.VMEM((max(32, 2 * rows), sz.left), F32),
                pltpu.VMEM((2, half, 2 * rows, sz.width), F32),
            ],
            compiler_params=params(SCOPE),
            name="site_" + str(step),
        )(bits, scales, *messages, *held, *fin)
        outs = [in_vmem(x) for x in outs]
        fin = outs[-2:]
        if not last:
            keep, give = outs[:2]

    sums = add(fin[0], swap_cores(fin[1]), False)
    parts = [to_pair(x, m) for m, x in zip(sz.inner, sums)] + [in_vmem(sums[-1])]
    tail = pl.pallas_call(
        functools.partial(norm_kernel, sz),
        out_shape=pltpu.VMEM((2, sz.extra), F32),
        in_specs=[VMEM] * half,
        out_specs=VMEM,
        compiler_params=params(2 * MIB),
        name="norms",
    )(*parts)
    tail = pl.pallas_call(
        sum_kernel,
        out_shape=pltpu.VMEM((2, sz.extra), F32),
        in_specs=[VMEM] * 2,
        out_specs=VMEM,
        compiler_params=params(MIB),
        name="norms_pair",
    )(in_vmem(tail), swap_cores(tail))
    parts = [in_vmem(tail)] + [to_pair(tail, m) for m in sz.inner]
    probs = pl.pallas_call(
        functools.partial(final_kernel, sz),
        out_shape=shape_of(1, sz.rows),
        in_specs=[VMEM] * (1 + half),
        out_specs=VMEM,
        compiler_params=params(MIB),
        name="probs",
    )(order, *parts)
    return probs.reshape(sz.rows, 1)


def solution(mesh):
    return jax.shard_map(
        on_device,
        mesh=mesh,
        in_specs=(P("seg", None, "bond", None), P("bond"), P(None, "seg"), P()),
        out_specs=P(None, "seg"),
        check_vma=False,
    )
```
